32 devices in a mesh: space: 4 (over z), batch: 8 (over y, x, core).
Axes of the slice: x: 2, y: 2, z: 4, core: 2. Of those that a mesh axis runs over, the one named last changes fastest.
Arguments:
- volume: bfloat16 [8, 4, 32, 32, 128], P('batch', None, 'space'), may hold values from -6 to 6
- kernel: bfloat16 [32, 108], replicated, may hold values from -0.625 to 0.625
- bias: float32 [32], replicated, may hold values from -3 to 3
- cotangent: bfloat16 [8, 32, 16, 1024], P('batch', 'space'), may hold values from -0.3515625 to 0.3515625
Outputs:
- pooled: bfloat16 [8, 32, 16, 1024], P('batch', 'space')
- kernel_grad: float32 [32, 108], replicated
- bias_grad: float32 [32], replicated
The draws below stay inside these ranges and needn't reach their ends.
All inputs are finite; a program needn't handle non-finite values.
Results may differ from the reference program's by a relative error of at most 0.0065.
Values may be sent and summed in bfloat16 or wider, within the bound.
A program may use at most 64 MiB of HBM per device.

```python
import jax
import jax.numpy as jnp
from jax import lax

CIN = 4
C1 = 32
HEIGHT = 32
WIDTH = 128
SAMPLES = 8
DEPTH = 32
PDEPTH = 16
PPLANE = 1024


def draw_cotangent(key, part):
    shape = (SAMPLES, C1, PDEPTH, PPLANE)
    sample_rise = 10.0 ** (jnp.arange(SAMPLES, dtype=jnp.float32) / max(SAMPLES - 1, 1))
    depth_rise = 3.0 ** (jnp.arange(PDEPTH, dtype=jnp.float32) / max(PDEPTH - 1, 1))
    factor = sample_rise[:, None, None, None] * depth_rise[None, None, :, None]
    scale = 2.0 / (8.0 * SAMPLES * PDEPTH * PPLANE) ** 0.5
    base = jnp.clip(jax.random.normal(key, shape, jnp.float32), -6.0, 6.0)
    return (base * factor * scale).astype(jnp.bfloat16)


def block_levels(stream_key, shape, split, least, largest):
    loudness, own = 1.0, jax.random.fold_in(stream_key, 6)
    for dim, shards_of in split:
        heights = jnp.exp(jax.random.uniform(jax.random.fold_in(own, dim), (shards_of,), jnp.float32, least / len(split), largest / len(split)))
        loudness = loudness * jnp.repeat(heights, shape[dim] // shards_of).reshape([-1 if axis == dim else 1 for axis in range(len(shape))])
    return loudness


def bell_draw(stream_key, shape, deviation, most, shards=(), kind=jnp.bfloat16):
    gain = block_levels(stream_key, shape, shards, -0.22, 0.18) if shards else 1.0
    entries = jax.random.normal(stream_key, shape, jnp.float32) * deviation * gain
    return jnp.minimum(jnp.maximum(entries, -most), most).astype(kind)


def setup_inputs(seed: int = 0) -> dict:
    key_of = jax.random.split(jax.random.key(seed), 5)
    return {
        "volume": bell_draw(key_of[0], (SAMPLES, CIN, DEPTH, HEIGHT, WIDTH), 1.0, 6.0, ((0, 8), (2, 4))),
        "kernel": bell_draw(key_of[1], (C1, 27 * CIN), (27 * CIN) ** -0.5, 0.625),
        "bias": bell_draw(key_of[2], (C1,), 0.5, 3.0, (), jnp.float32),
        "cotangent": draw_cotangent(jax.random.fold_in(key_of[4], 71), 0),
    }


def reference(volume, kernel, bias, cotangent):
    filters = kernel.astype(jnp.float32).reshape(C1, 3, 3, 3, CIN).transpose(0, 4, 1, 2, 3)

    def one_sample(pair):
        sample_volume, sample_cot = pair
        as_float = sample_volume.astype(jnp.float32)
        conv_out = lax.conv_general_dilated(as_float[None], filters, (1, 1, 1), ((1, 1), (1, 1), (1, 1)),
                                            dimension_numbers=("NCDHW", "OIDHW", "NCDHW"),
                                            precision=lax.Precision.HIGHEST)[0]
        conv_out = conv_out + bias[:, None, None, None]
        positive = conv_out > 0
        activated = jnp.where(positive, conv_out, 0.3 * conv_out).astype(jnp.bfloat16)
        pooled = activated.astype(jnp.float32).reshape(C1, DEPTH // 2, 2, HEIGHT // 2, 2, WIDTH // 2, 2)
        pooled = pooled.mean(axis=(2, 4, 6)).astype(jnp.bfloat16).reshape(C1, DEPTH // 2, PPLANE)
        incoming = sample_cot.astype(jnp.float32).reshape(C1, DEPTH // 2, 1, HEIGHT // 2, 1, WIDTH // 2, 1) * 0.125
        widened = jnp.broadcast_to(incoming, (C1, DEPTH // 2, 2, HEIGHT // 2, 2, WIDTH // 2, 2)).reshape(C1, DEPTH, HEIGHT, WIDTH)
        spread = (widened * jnp.where(positive, 1.0, 0.3)).astype(jnp.bfloat16).astype(jnp.float32)
        padded = jnp.pad(as_float, ((0, 0), (1, 1), (1, 1), (1, 1)))
        pieces = []
        for shift_d in range(3):
            for shift_h in range(3):
                for shift_w in range(3):
                    shifted = padded[:, shift_d:shift_d + DEPTH, shift_h:shift_h + HEIGHT, shift_w:shift_w + WIDTH]
                    pieces.append(jnp.einsum("odhw,cdhw->oc", spread, shifted, precision=lax.Precision.HIGHEST))
        kernel_part = jnp.stack(pieces, axis=1).reshape(C1, 27 * CIN)
        return pooled, kernel_part, jnp.sum(spread, axis=(1, 2, 3))

    pooled, kernel_parts, bias_parts = lax.map(one_sample, (volume, cotangent))
    return pooled, jnp.sum(kernel_parts, axis=0), jnp.sum(bias_parts, axis=0)
```

```python
import functools

import jax
import jax.numpy as jnp
from jax import lax
from jax.experimental import pallas as pl
from jax.experimental.pallas import tpu as pltpu
from jax.sharding import PartitionSpec as P

MESH = pl.DeviceIdType.MESH
F32, BF16, I32 = jnp.float32, jnp.bfloat16, jnp.int32


def iota(shape, dim):
    return lax.broadcasted_iota(I32, shape, dim)


def onehot(rows, columns, source, value=1.0):
    return jnp.where(
        iota((rows, columns), 1) == source(iota((rows, columns), 0)), value, 0.0
    ).astype(BF16)


def fused_kernel(
    dims, vol_ref, ker_ref, bias_ref, cot_ref, pooled_ref, kg_ref, bg_ref,
    halo_lo, halo_hi, planes, patches, signs, cot_send, cot_recv, pool_flat,
    pool_send, pool_recv, part_recv, row_recv,
    halo_ssem, halo_rsem, cot_ssem, cot_rsem, pool_ssem, pool_rsem,
    part_ssem, part_rsem, row_ssem, row_rsem,
):
    spaces, batches, cin, slab, height, breadth, filters, group, pdepth, plane = dims
    local = slab // 2
    rows = local * filters
    block_rows = local * group
    groups = slab // 2 + 1
    kdim = 64 * cin
    taps = 27 * cin
    z = lax.axis_index("space")
    b = lax.axis_index("batch")

    barrier = pltpu.get_barrier_semaphore()
    for k in range(1, spaces):
        pl.semaphore_signal(
            barrier, inc=1, device_id={"space": lax.rem(z + k, spaces)}, device_id_type=MESH
        )
    for k in range(1, batches):
        pl.semaphore_signal(
            barrier, inc=1, device_id={"batch": lax.rem(b + k, batches)}, device_id_type=MESH
        )

    def by_slab(r):
        s = r // block_rows
        p = (r // group) % local
        return (r % group) * pdepth + s * local + p

    cotangent = cot_ref[0].reshape(rows, plane)
    cot_send[...] = (
        jnp.dot(onehot(rows, rows, by_slab), cotangent, preferred_element_type=F32)
        .astype(BF16)
        .reshape(spaces, block_rows, plane)
    )
    pl.semaphore_wait(barrier, spaces + batches - 2)

    up = pltpu.make_async_remote_copy(
        src_ref=vol_ref.at[0, :, slab - 1], dst_ref=halo_lo,
        send_sem=halo_ssem.at[0], recv_sem=halo_rsem.at[0],
        device_id={"space": lax.rem(z + 1, spaces)}, device_id_type=MESH,
    )
    down = pltpu.make_async_remote_copy(
        src_ref=vol_ref.at[0, :, 0], dst_ref=halo_hi,
        send_sem=halo_ssem.at[1], recv_sem=halo_rsem.at[1],
        device_id={"space": lax.rem(z + spaces - 1, spaces)}, device_id_type=MESH,
    )

    @pl.when(z < spaces - 1)
    def _():
        up.start()

    @pl.when(z > 0)
    def _():
        down.start()

    def exchange(send, recv, ssem, rsem):
        copies = []
        for k in range(1, spaces):
            to = lax.rem(z + k, spaces)
            copies.append(
                pltpu.make_async_remote_copy(
                    src_ref=send.at[to], dst_ref=recv.at[z],
                    send_sem=ssem.at[k], recv_sem=rsem.at[k],
                    device_id={"space": to}, device_id_type=MESH,
                )
            )
        return copies

    cot_copies = exchange(cot_send, cot_recv, cot_ssem, cot_rsem)
    for copy in cot_copies:
        copy.start()
    cot_recv[z] = cot_send[z]

    def spread_tap(lane):
        bb, ee, aa = lane // (16 * cin), (lane // (4 * cin)) % 4, (lane // cin) % 4
        inside = (aa < 3) & (bb < 3) & (ee < 3)
        return jnp.where(inside, (aa * 9 + bb * 3 + ee) * cin + lane % cin, -1)

    place = jnp.where(
        iota((taps, kdim), 0) == spread_tap(iota((taps, kdim), 1)), 1.0, 0.0
    ).astype(BF16)
    base = jnp.dot(ker_ref[...], place, preferred_element_type=F32)
    parities = [(pd, ph, pw) for pd in range(2) for ph in range(2) for pw in range(2)]
    shifts = [ph * 16 * cin + pw * 4 * cin + pd * cin for pd, ph, pw in parities]
    weights = jnp.concatenate(
        [base if s == 0 else pltpu.roll(base, s, 1) for s in shifts], axis=0
    ).astype(BF16)
    bias = jnp.sum(
        jnp.where(iota((filters, filters), 0) == iota((filters, filters), 1), bias_ref[...], 0.0),
        axis=1, keepdims=True,
    )

    pair_rows = 2 * cin * height
    turn = onehot(
        pair_rows, pair_rows,
        lambda r: (r % cin) * (2 * height) + ((r // cin) % 2) * height + r // (2 * cin),
    )

    def pair(first, second):
        pieces = []
        for c in range(cin):
            pieces += [first(c), second(c)]
        return jnp.concatenate(pieces, axis=0)

    def own(d):
        return lambda c: vol_ref[0, c, d]

    def turned(pairs):
        out = jnp.dot(turn, jnp.concatenate(pairs, axis=1), preferred_element_type=F32)
        return [
            out[:, i * breadth : (i + 1) * breadth].reshape(height, 2 * cin, breadth)
            for i in range(len(pairs))
        ]

    inner = turned([pair(own(2 * g - 1), own(2 * g)) for g in range(1, groups - 1)])

    @pl.when(z > 0)
    def _():
        up.wait_recv()

    @pl.when(z == 0)
    def _():
        halo_lo[...] = jnp.zeros_like(halo_lo)

    @pl.when(z < spaces - 1)
    def _():
        down.wait_recv()

    @pl.when(z == spaces - 1)
    def _():
        halo_hi[...] = jnp.zeros_like(halo_hi)

    outer = turned([pair(lambda c: halo_lo[c], own(0)), pair(own(slab - 1), lambda c: halo_hi[c])])
    all_groups = [outer[0], *inner, outer[1]]
    stack = planes.shape[1]
    if stack > groups * 2 * cin:
        all_groups.append(jnp.zeros((height, stack - groups * 2 * cin, breadth), F32))
    planes[0] = jnp.zeros((stack, breadth), BF16)
    planes[height + 1] = jnp.zeros((stack, breadth), BF16)
    planes[1 : height + 1] = jnp.concatenate(all_groups, axis=1).astype(BF16)

    half = breadth // 2

    def split_lane(lane):
        we, side, j = lane // breadth, (lane // half) % 2, lane % half
        w = 2 * j + we - 1
        return jnp.where((w >= 0) & (w < breadth), side * breadth + w, -1)

    select = jnp.where(
        iota((2 * breadth, 4 * breadth), 0) == split_lane(iota((2 * breadth, 4 * breadth), 1)),
        1.0, 0.0,
    ).astype(BF16)
    tiles = height // 4
    krows = 4 * cin
    for wh in range(4):
        left = jnp.concatenate(
            [
                jnp.concatenate([planes[4 * t + wh], planes[4 * t + wh + 2]], axis=1)
                for t in range(tiles)
            ],
            axis=0,
        )
        picked = jnp.dot(left, select, preferred_element_type=F32)
        for t in range(tiles):
            for we in range(4):
                for p in range(local):
                    start = t * stack + p * 2 * cin
                    patches[
                        p, (wh * 4 + we) * krows : (wh * 4 + we + 1) * krows,
                        t * breadth : (t + 1) * breadth,
                    ] = picked[start : start + krows, we * breadth : (we + 1) * breadth].astype(BF16)

    step = 256
    chunks = plane // step
    for p in range(local):
        for n in range(chunks):
            lanes = slice(n * step, (n + 1) * step)
            conv = jnp.dot(weights, patches[p, :, lanes], preferred_element_type=F32)
            total = None
            for i in range(8):
                part = conv[i * filters : (i + 1) * filters] + bias
                signs[p, i * filters : (i + 1) * filters, lanes] = part.astype(BF16)
                active = jnp.maximum(part, 0.3 * part)
                total = active if total is None else total + active
            pool_flat[p * filters : (p + 1) * filters, lanes] = (total * 0.125).astype(BF16)

    def by_owner(r):
        s = r // block_rows
        p = (r // group) % local
        return p * filters + s * group + r % group

    pool_send[...] = (
        jnp.dot(onehot(rows, rows, by_owner), pool_flat[...], preferred_element_type=F32)
        .astype(BF16)
        .reshape(spaces, block_rows, plane)
    )
    pool_copies = exchange(pool_send, pool_recv, pool_ssem, pool_rsem)
    for copy in pool_copies:
        copy.start()
    pool_recv[z] = pool_send[z]

    for copy in cot_copies:
        copy.wait_recv()

    def by_depth(r):
        p, o = r // filters, r % filters
        return (o // group) * block_rows + p * group + o % group

    u = jnp.dot(
        onehot(rows, rows, by_depth, 0.125), cot_recv[...].reshape(rows, plane),
        preferred_element_type=F32,
    )
    low = (0.3 * u).astype(BF16).astype(F32)
    grad = jnp.zeros((8 * filters, kdim), F32)
    bias_sum = jnp.zeros((filters, step), F32)
    for p in range(local):
        for n in range(chunks):
            lanes = slice(n * step, (n + 1) * step)
            up_value = u[p * filters : (p + 1) * filters, lanes]
            low_value = low[p * filters : (p + 1) * filters, lanes]
            spread = []
            for i in range(8):
                sign = signs[p, i * filters : (i + 1) * filters, lanes].astype(F32)
                one = jnp.where(sign > 0, up_value, low_value)
                bias_sum = bias_sum + one
                spread.append(one.astype(BF16))
            grad = grad + lax.dot_general(
                jnp.concatenate(spread, axis=0), patches[p, :, lanes],
                (((1,), (1,)), ((), ())), preferred_element_type=F32,
            )

    folded = None
    for i, s in enumerate(shifts):
        part = grad[i * filters : (i + 1) * filters]
        part = part if s == 0 else pltpu.roll(part, kdim - s, 1)
        folded = part if folded is None else folded + part
    width = part_recv.shape[2]
    collect = jnp.where(
        iota((kdim, width), 1) == spread_tap(iota((kdim, width), 0)), 1.0, 0.0
    )
    compact = jnp.dot(
        folded, collect, preferred_element_type=F32, precision=lax.Precision.HIGHEST
    )
    bias_column = jnp.sum(bias_sum, axis=1, keepdims=True)
    part_recv[b] = compact + jnp.where(iota((filters, width), 1) == taps, bias_column, 0.0)

    part_copies = []
    for k in range(1, batches):
        part_copies.append(
            pltpu.make_async_remote_copy(
                src_ref=part_recv.at[b], dst_ref=part_recv.at[b],
                send_sem=part_ssem.at[k], recv_sem=part_rsem.at[k],
                device_id={"batch": lax.rem(b + k, batches)}, device_id_type=MESH,
            )
        )
    for copy in part_copies:
        copy.start()
    for copy in part_copies:
        copy.wait_recv()
    total = part_recv[0]
    for k in range(1, batches):
        total = total + part_recv[k]
    row_recv[z] = total
    row_copies = []
    for k in range(1, spaces):
        row_copies.append(
            pltpu.make_async_remote_copy(
                src_ref=row_recv.at[z], dst_ref=row_recv.at[z],
                send_sem=row_ssem.at[k], recv_sem=row_rsem.at[k],
                device_id={"space": lax.rem(z + k, spaces)}, device_id_type=MESH,
            )
        )
    for copy in row_copies:
        copy.start()

    for copy in pool_copies:
        copy.wait_recv()

    def by_channel(r):
        ol, s, p = r // pdepth, (r // local) % spaces, r % local
        return s * block_rows + p * group + ol

    pooled_ref[0] = (
        jnp.dot(
            onehot(rows, rows, by_channel), pool_recv[...].reshape(rows, plane),
            preferred_element_type=F32,
        )
        .astype(BF16)
        .reshape(group, pdepth, plane)
    )

    for copy in row_copies:
        copy.wait_recv()
    total = row_recv[0]
    for k in range(1, spaces):
        total = total + row_recv[k]
    kg_ref[...] = total[:, :taps]
    bg_ref[...] = jnp.sum(
        jnp.where(
            iota((filters, filters), 0) == iota((filters, filters), 1),
            total[:, taps : taps + 1], 0.0,
        ),
        axis=0, keepdims=True,
    )

    @pl.when(z < spaces - 1)
    def _():
        up.wait_send()

    @pl.when(z > 0)
    def _():
        down.wait_send()

    for copy in cot_copies + pool_copies + part_copies + row_copies:
        copy.wait_send()


def solution(mesh):
    spaces, batches = mesh.shape["space"], mesh.shape["batch"]

    def on_device(volume, kernel, bias, cotangent):
        _, cin, slab, height, breadth = volume.shape
        filters = kernel.shape[0]
        _, group, pdepth, plane = cotangent.shape
        taps = kernel.shape[1]
        width = -(-(taps + 1) // 128) * 128
        local = slab // 2
        block = (spaces, local * group, plane)
        stack = -(-((slab + 2) * cin) // 16) * 16
        dma = pltpu.SemaphoreType.DMA
        vmem = pl.BlockSpec(memory_space=pltpu.VMEM)
        pooled, kernel_grad, bias_grad = pl.pallas_call(
            functools.partial(
                fused_kernel,
                (spaces, batches, cin, slab, height, breadth, filters, group, pdepth, plane),
            ),
            out_shape=(
                jax.ShapeDtypeStruct(cotangent.shape, BF16),
                jax.ShapeDtypeStruct(kernel.shape, F32),
                jax.ShapeDtypeStruct((1, filters), F32),
            ),
            in_specs=[vmem] * 4,
            out_specs=(vmem, vmem, vmem),
            scratch_shapes=[
                pltpu.VMEM((cin, height, breadth), BF16),
                pltpu.VMEM((cin, height, breadth), BF16),
                pltpu.VMEM((height + 2, stack, breadth), BF16),
                pltpu.VMEM((local, 64 * cin, plane), BF16),
                pltpu.VMEM((local, 8 * filters, plane), BF16),
                pltpu.VMEM(block, BF16),
                pltpu.VMEM(block, BF16),
                pltpu.VMEM((local * filters, plane), BF16),
                pltpu.VMEM(block, BF16),
                pltpu.VMEM(block, BF16),
                pltpu.VMEM((batches, filters, width), F32),
                pltpu.VMEM((spaces, filters, width), F32),
                dma((2,)), dma((2,)),
                dma((spaces,)), dma((spaces,)),
                dma((spaces,)), dma((spaces,)),
                dma((batches,)), dma((batches,)),
                dma((spaces,)), dma((spaces,)),
            ],
            compiler_params=pltpu.CompilerParams(
                collective_id=0, has_side_effects=True, vmem_limit_bytes=40 * 2**20
            ),
        )(volume, kernel, bias.reshape(1, filters), cotangent)
        return pooled, kernel_grad, bias_grad.reshape(filters)

    placed = (P("batch", None, "space", None, None), P(), P(), P("batch", "space", None, None))
    return jax.shard_map(
        on_device,
        mesh=mesh,
        in_specs=placed,
        out_specs=(P("batch", "space", None, None), P(), P()),
        check_vma=False,
    )
```

```python
import functools

import jax
import jax.numpy as jnp
from jax import lax
from jax.experimental import pallas as pl
from jax.experimental.pallas import tpu as pltpu
from jax.sharding import PartitionSpec as P

MESH = pl.DeviceIdType.MESH
LIMIT = 63 * 2**20
F32, BF16, I32 = jnp.float32, jnp.bfloat16, jnp.int32


def iota(shape, dim):
    return lax.broadcasted_iota(I32, shape, dim)


def onehot(rows, columns, source, value=1.0):
    return jnp.where(
        iota((rows, columns), 1) == source(iota((rows, columns), 0)), value, 0.0
    ).astype(BF16)


def fused_kernel(
    dims, vol_hbm, ker_hbm, bias_hbm, cot_hbm, pooled_out, kg_out, bg_out,
    vol_ref, ker_ref, bias_ref, cot_ref, in_sem, halo_lo, halo_hi, planes, planes_in, patches, signs, cot_send, cot_recv, pool_flat,
    pool_send, pool_recv, part_recv, row_recv, pooled_ref, kg_ref, bg_ref, out_sem,
    halo_ssem, halo_rsem, cot_ssem, cot_rsem, pool_ssem, pool_rsem,
    part_ssem, part_rsem, row_ssem, row_rsem,
):
    spaces, batches, cin, slab, height, breadth, filters, group, pdepth, plane = dims
    local = slab // 2
    rows = local * filters
    block_rows = local * group
    groups = slab // 2 + 1
    kdim = 64 * cin
    taps = 27 * cin
    z = lax.axis_index("space")
    b = lax.axis_index("batch")

    loads = [
        pltpu.make_async_copy(source, target, in_sem.at[i])
        for i, (source, target) in enumerate(
            [(cot_hbm, cot_ref), (vol_hbm, vol_ref), (ker_hbm, ker_ref), (bias_hbm, bias_ref)]
        )
    ]
    for load in loads:
        load.start()

    barrier = pltpu.get_barrier_semaphore()
    for k in range(1, spaces):
        pl.semaphore_signal(
            barrier, inc=1, device_id={"space": lax.rem(z + k, spaces)}, device_id_type=MESH
        )
    for k in range(1, batches):
        pl.semaphore_signal(
            barrier, inc=1, device_id={"batch": lax.rem(b + k, batches)}, device_id_type=MESH
        )

    def by_slab(r):
        s = r // block_rows
        p = (r // group) % local
        return (r % group) * pdepth + s * local + p

    loads[0].wait()
    cotangent = cot_ref[0].reshape(rows, plane)
    cot_send[...] = (
        jnp.dot(onehot(rows, rows, by_slab), cotangent, preferred_element_type=F32)
        .astype(BF16)
        .reshape(spaces, block_rows, plane)
    )
    pl.semaphore_wait(barrier, spaces + batches - 2)

    up = pltpu.make_async_remote_copy(
        src_ref=vol_hbm.at[0, :, slab - 1], dst_ref=halo_lo,
        send_sem=halo_ssem.at[0], recv_sem=halo_rsem.at[0],
        device_id={"space": lax.rem(z + 1, spaces)}, device_id_type=MESH,
    )
    down = pltpu.make_async_remote_copy(
        src_ref=vol_hbm.at[0, :, 0], dst_ref=halo_hi,
        send_sem=halo_ssem.at[1], recv_sem=halo_rsem.at[1],
        device_id={"space": lax.rem(z + spaces - 1, spaces)}, device_id_type=MESH,
    )

    @pl.when(z < spaces - 1)
    def _():
        up.start()

    @pl.when(z > 0)
    def _():
        down.start()

    def exchange(send, recv, ssem, rsem):
        copies = []
        for k in range(1, spaces):
            to = lax.rem(z + k, spaces)
            copies.append(
                pltpu.make_async_remote_copy(
                    src_ref=send.at[to], dst_ref=recv.at[z],
                    send_sem=ssem.at[k], recv_sem=rsem.at[k],
                    device_id={"space": to}, device_id_type=MESH,
                )
            )
        return copies

    cot_copies = exchange(cot_send, cot_recv, cot_ssem, cot_rsem)
    for copy in cot_copies:
        copy.start()
    cot_recv[z] = cot_send[z]

    def spread_tap(lane):
        bb, ee, aa = lane // (16 * cin), (lane // (4 * cin)) % 4, (lane // cin) % 4
        inside = (aa < 3) & (bb < 3) & (ee < 3)
        return jnp.where(inside, (aa * 9 + bb * 3 + ee) * cin + lane % cin, -1)

    for load in loads[1:]:
        load.wait()
    place = jnp.where(
        iota((taps, kdim), 0) == spread_tap(iota((taps, kdim), 1)), 1.0, 0.0
    ).astype(BF16)
    base = jnp.dot(ker_ref[...], place, preferred_element_type=F32)
    parities = [(pd, ph, pw) for pd in range(2) for ph in range(2) for pw in range(2)]
    shifts = [ph * 16 * cin + pw * 4 * cin + pd * cin for pd, ph, pw in parities]
    weights = jnp.concatenate(
        [base if s == 0 else pltpu.roll(base, s, 1) for s in shifts], axis=0
    ).astype(BF16)
    bias = jnp.sum(
        jnp.where(iota((filters, filters), 0) == iota((filters, filters), 1), bias_ref[...], 0.0),
        axis=1, keepdims=True,
    )

    pair_rows = 2 * cin * height
    turn = onehot(
        pair_rows, pair_rows,
        lambda r: (r % cin) * (2 * height) + ((r // cin) % 2) * height + r // (2 * cin),
    )

    def pair(first, second):
        pieces = []
        for c in range(cin):
            pieces += [first(c), second(c)]
        return jnp.concatenate(pieces, axis=0)

    def own(d):
        return lambda c: vol_ref[0, c, d]

    def turned(pairs):
        out = jnp.dot(turn, jnp.concatenate(pairs, axis=1), preferred_element_type=F32)
        return [
            out[:, i * breadth : (i + 1) * breadth].reshape(height, 2 * cin, breadth)
            for i in range(len(pairs))
        ]

    inner = turned([pair(own(2 * g - 1), own(2 * g)) for g in range(1, groups - 1)])

    half = breadth // 2

    def split_lane(lane):
        we, side, j = lane // breadth, (lane // half) % 2, lane % half
        w = 2 * j + we - 1
        return jnp.where((w >= 0) & (w < breadth), side * breadth + w, -1)

    select = jnp.where(
        iota((2 * breadth, 4 * breadth), 0) == split_lane(iota((2 * breadth, 4 * breadth), 1)),
        1.0, 0.0,
    ).astype(BF16)
    tiles = height // 4
    krows = 4 * cin
    step = 256
    chunks = plane // step

    def forward(held, members, depths):
        stack = held.shape[1]
        members = list(members)
        if stack > len(members) * 2 * cin:
            members.append(jnp.zeros((height, stack - len(members) * 2 * cin, breadth), F32))
        held[0] = jnp.zeros((stack, breadth), BF16)
        held[height + 1] = jnp.zeros((stack, breadth), BF16)
        held[1 : height + 1] = jnp.concatenate(members, axis=1).astype(BF16)
        for wh in range(4):
            left = jnp.concatenate(
                [
                    jnp.concatenate([held[4 * t + wh], held[4 * t + wh + 2]], axis=1)
                    for t in range(tiles)
                ],
                axis=0,
            )
            picked = jnp.dot(left, select, preferred_element_type=F32)
            for t in range(tiles):
                for we in range(4):
                    for p, first in depths:
                        start = t * stack + first * 2 * cin
                        patches[
                            p, (wh * 4 + we) * krows : (wh * 4 + we + 1) * krows,
                            t * breadth : (t + 1) * breadth,
                        ] = picked[
                            start : start + krows, we * breadth : (we + 1) * breadth
                        ].astype(BF16)
        for p, _ in depths:
            for n in range(chunks):
                lanes = slice(n * step, (n + 1) * step)
                conv = jnp.dot(weights, patches[p, :, lanes], preferred_element_type=F32)
                total = None
                for i in range(8):
                    part = conv[i * filters : (i + 1) * filters] + bias
                    signs[p, i * filters : (i + 1) * filters, lanes] = part.astype(BF16)
                    active = jnp.maximum(part, 0.3 * part)
                    total = active if total is None else total + active
                pool_flat[p * filters : (p + 1) * filters, lanes] = (total * 0.125).astype(BF16)

    if local > 2:
        forward(planes_in, inner, [(p, p - 1) for p in range(1, local - 1)])

    @pl.when(z > 0)
    def _():
        up.wait_recv()

    @pl.when(z == 0)
    def _():
        halo_lo[...] = jnp.zeros_like(halo_lo)

    @pl.when(z < spaces - 1)
    def _():
        down.wait_recv()

    @pl.when(z == spaces - 1)
    def _():
        halo_hi[...] = jnp.zeros_like(halo_hi)

    outer = turned([pair(lambda c: halo_lo[c], own(0)), pair(own(slab - 1), lambda c: halo_hi[c])])
    forward(planes, [outer[0], inner[0], inner[-1], outer[1]], [(0, 0), (local - 1, 2)])

    def by_owner(r):
        s = r // block_rows
        p = (r // group) % local
        return p * filters + s * group + r % group

    pool_send[...] = (
        jnp.dot(onehot(rows, rows, by_owner), pool_flat[...], preferred_element_type=F32)
        .astype(BF16)
        .reshape(spaces, block_rows, plane)
    )
    pool_copies = exchange(pool_send, pool_recv, pool_ssem, pool_rsem)
    for copy in pool_copies:
        copy.start()
    pool_recv[z] = pool_send[z]

    for copy in cot_copies:
        copy.wait_recv()

    def by_depth(r):
        p, o = r // filters, r % filters
        return (o // group) * block_rows + p * group + o % group

    u = jnp.dot(
        onehot(rows, rows, by_depth, 0.125), cot_recv[...].reshape(rows, plane),
        preferred_element_type=F32,
    )
    low = (0.3 * u).astype(BF16).astype(F32)
    grad = jnp.zeros((8 * filters, kdim), F32)
    bias_sum = jnp.zeros((filters, step), F32)
    for p in range(local):
        for n in range(chunks):
            lanes = slice(n * step, (n + 1) * step)
            up_value = u[p * filters : (p + 1) * filters, lanes]
            low_value = low[p * filters : (p + 1) * filters, lanes]
            spread = []
            for i in range(8):
                sign = signs[p, i * filters : (i + 1) * filters, lanes].astype(F32)
                one = jnp.where(sign > 0, up_value, low_value)
                bias_sum = bias_sum + one
                spread.append(one.astype(BF16))
            grad = grad + lax.dot_general(
                jnp.concatenate(spread, axis=0), patches[p, :, lanes],
                (((1,), (1,)), ((), ())), preferred_element_type=F32,
            )

    folded = None
    for i, s in enumerate(shifts):
        part = grad[i * filters : (i + 1) * filters]
        part = part if s == 0 else pltpu.roll(part, kdim - s, 1)
        folded = part if folded is None else folded + part
    width = part_recv.shape[2]
    collect = jnp.where(
        iota((kdim, width), 1) == spread_tap(iota((kdim, width), 0)), 1.0, 0.0
    )
    compact = jnp.dot(
        folded, collect, preferred_element_type=F32, precision=lax.Precision.HIGHEST
    )
    bias_column = jnp.sum(bias_sum, axis=1, keepdims=True)
    part_recv[b] = compact + jnp.where(iota((filters, width), 1) == taps, bias_column, 0.0)

    part_copies = []
    for k in range(1, batches):
        part_copies.append(
            pltpu.make_async_remote_copy(
                src_ref=part_recv.at[b], dst_ref=part_recv.at[b],
                send_sem=part_ssem.at[k], recv_sem=part_rsem.at[k],
                device_id={"batch": lax.rem(b + k, batches)}, device_id_type=MESH,
            )
        )
    for copy in part_copies:
        copy.start()
    for copy in part_copies:
        copy.wait_recv()
    total = part_recv[0]
    for k in range(1, batches):
        total = total + part_recv[k]
    row_recv[z] = total
    row_copies = []
    for k in range(1, spaces):
        row_copies.append(
            pltpu.make_async_remote_copy(
                src_ref=row_recv.at[z], dst_ref=row_recv.at[z],
                send_sem=row_ssem.at[k], recv_sem=row_rsem.at[k],
                device_id={"space": lax.rem(z + k, spaces)}, device_id_type=MESH,
            )
        )
    for copy in row_copies:
        copy.start()

    stores = [
        pltpu.make_async_copy(source, target, out_sem.at[i])
        for i, (source, target) in enumerate(
            [(kg_ref, kg_out), (bg_ref, bg_out), (pooled_ref, pooled_out)]
        )
    ]
    for copy in pool_copies:
        copy.wait_recv()

    def by_channel(r):
        ol, s, p = r // pdepth, (r // local) % spaces, r % local
        return s * block_rows + p * group + ol

    pooled_ref[0] = (
        jnp.dot(
            onehot(rows, rows, by_channel), pool_recv[...].reshape(rows, plane),
            preferred_element_type=F32,
        )
        .astype(BF16)
        .reshape(group, pdepth, plane)
    )
    stores[2].start()

    for copy in row_copies:
        copy.wait_recv()
    total = row_recv[0]
    for k in range(1, spaces):
        total = total + row_recv[k]
    kg_ref[...] = total[:, :taps]
    bg_ref[...] = jnp.sum(
        jnp.where(
            iota((filters, filters), 0) == iota((filters, filters), 1),
            total[:, taps : taps + 1], 0.0,
        ),
        axis=0, keepdims=True,
    )
    stores[0].start()
    stores[1].start()

    @pl.when(z < spaces - 1)
    def _():
        up.wait_send()

    @pl.when(z > 0)
    def _():
        down.wait_send()

    for copy in cot_copies + pool_copies + part_copies + row_copies:
        copy.wait_send()
    for store in stores:
        store.wait()


def finish_kernel(*refs):
    count = (len(refs) - 1) // 2
    copies = [
        pltpu.make_async_copy(refs[i], refs[count + i], refs[-1].at[i]) for i in range(count)
    ]
    for copy in copies:
        copy.start()
    for copy in copies:
        copy.wait()


def solution(mesh):
    spaces, batches = mesh.shape["space"], mesh.shape["batch"]

    def on_device(volume, kernel, bias, cotangent):
        _, cin, slab, height, breadth = volume.shape
        filters = kernel.shape[0]
        _, group, pdepth, plane = cotangent.shape
        taps = kernel.shape[1]
        width = -(-(taps + 1) // 128) * 128
        local = slab // 2
        block = (spaces, local * group, plane)
        stack = -(-(max(local - 1, 1) * 2 * cin) // 16) * 16
        dma = pltpu.SemaphoreType.DMA
        hbm = pl.BlockSpec(memory_space=pltpu.HBM)
        shapes = (
            jax.ShapeDtypeStruct(cotangent.shape, BF16),
            jax.ShapeDtypeStruct(kernel.shape, F32),
            jax.ShapeDtypeStruct((1, filters), F32),
        )
        results = pl.pallas_call(
            functools.partial(
                fused_kernel,
                (spaces, batches, cin, slab, height, breadth, filters, group, pdepth, plane),
            ),
            out_shape=shapes,
            in_specs=[hbm] * 4,
            out_specs=(hbm,) * 3,
            scratch_shapes=[
                pltpu.VMEM(volume.shape, BF16),
                pltpu.VMEM(kernel.shape, BF16),
                pltpu.VMEM((1, filters), F32),
                pltpu.VMEM(cotangent.shape, BF16),
                dma((4,)),
                pltpu.VMEM((cin, height, breadth), BF16),
                pltpu.VMEM((cin, height, breadth), BF16),
                pltpu.VMEM((height + 2, 8 * cin, breadth), BF16),
                pltpu.VMEM((height + 2, stack, breadth), BF16),
                pltpu.VMEM((local, 64 * cin, plane), BF16),
                pltpu.VMEM((local, 8 * filters, plane), BF16),
                pltpu.VMEM(block, BF16),
                pltpu.VMEM(block, BF16),
                pltpu.VMEM((local * filters, plane), BF16),
                pltpu.VMEM(block, BF16),
                pltpu.VMEM(block, BF16),
                pltpu.VMEM((batches, filters, width), F32),
                pltpu.VMEM((spaces, filters, width), F32),
                pltpu.VMEM(cotangent.shape, BF16),
                pltpu.VMEM(kernel.shape, F32),
                pltpu.VMEM((1, filters), F32),
                dma((3,)),
                dma((2,)), dma((2,)),
                dma((spaces,)), dma((spaces,)),
                dma((spaces,)), dma((spaces,)),
                dma((batches,)), dma((batches,)),
                dma((spaces,)), dma((spaces,)),
            ],
            compiler_params=pltpu.CompilerParams(
                collective_id=0, has_side_effects=True, vmem_limit_bytes=LIMIT
            ),
        )(volume, kernel, bias.reshape(1, filters), cotangent)
        pooled, kernel_grad, bias_grad = pl.pallas_call(
            finish_kernel,
            out_shape=shapes,
            in_specs=[hbm] * 3,
            out_specs=(hbm,) * 3,
            scratch_shapes=[dma((3,))],
            compiler_params=pltpu.CompilerParams(vmem_limit_bytes=LIMIT),
        )(*results)
        return pooled, kernel_grad, bias_grad.reshape(filters)

    placed = (P("batch", None, "space", None, None), P(), P(), P("batch", "space", None, None))
    return jax.shard_map(
        on_device,
        mesh=mesh,
        in_specs=placed,
        out_specs=(P("batch", "space", None, None), P(), P()),
        check_vma=False,
    )
```
